32 devices in a mesh: pair: 8 (over z, core), narrow: 4 (over y, x).
Axes of the slice: x: 2, y: 2, z: 4, core: 2. Of those that a mesh axis runs over, the one named last changes fastest.
Arguments:
- trial_slab: bfloat16 [8, 64, 10240], P(None, 'pair', 'narrow'), may hold values from -6 to 6
- ladder: bfloat16 [8192, 10240], P('pair', 'narrow'), may hold values from -0.0625 to 0.0625
- range_irreps: int32 [8], replicated, may hold values from 0 to 7, as said below
Outputs:
- sigma: bfloat16 [64, 8192], P(('pair', 'narrow'))
The draws below stay inside these ranges and needn't reach their ends.
Inputs may be any that keep to these rules, and one draw needn't show every extreme that they name: `range_irreps`: non-decreasing along the pair index; the first entry is 0 and the last is 7.
All inputs are finite; a program needn't handle non-finite values.
Results may differ from the reference program's by a relative error of at most 0.019.
Values may be sent and summed in bfloat16 or wider, within the bound.
A program may use at most 64 MiB of HBM per device.

```python
import jax
import jax.numpy as jnp
from jax import lax

CD = 10240
IRREPS = 8
AB_DEV = 1024
AB = 8192
ROWS = 64
N_PAIR = 8
N_NARROW = 4


def draw_range_irreps(key, part):
    inner = jax.random.randint(key, (N_PAIR - 2,), 0, IRREPS).astype(jnp.int32)
    first = jnp.zeros((1,), jnp.int32)
    last = jnp.full((1,), IRREPS - 1, jnp.int32)
    return jnp.sort(jnp.concatenate([first, inner, last]))


def steps_of(key, shape, shards, smallest, top_value):
    factor_of, own = 1.0, jax.random.fold_in(key, 6)
    for axis_at, blocks in shards:
        heights = jnp.exp(jax.random.uniform(jax.random.fold_in(own, axis_at), (blocks,), jnp.float32, smallest / len(shards), top_value / len(shards)))
        factor_of = factor_of * jnp.repeat(heights, shape[axis_at] // blocks).reshape([-1 if axis == axis_at else 1 for axis in range(len(shape))])
    return factor_of


def gaussian(rng, shape, deviation, reach, split=(), kind=jnp.bfloat16):
    loudness = steps_of(rng, shape, split, -0.22, 0.18) if split else 1.0
    array = jax.random.normal(rng, shape, jnp.float32) * deviation * loudness
    return jnp.minimum(jnp.maximum(array, -reach), reach).astype(kind)


def setup_inputs(seed: int = 0) -> dict:
    key_list = jax.random.split(jax.random.key(seed), 4)
    trial_slab = gaussian(key_list[0], (IRREPS, ROWS, CD), 1.0, 6.0, ((1, 8), (2, 4)))
    ladder = gaussian(key_list[1], (AB, CD), CD ** -0.5, 0.0625, ((0, 8), (1, 4)))
    range_irreps = draw_range_irreps(jax.random.fold_in(key_list[3], 71), 0)
    return dict(trial_slab=trial_slab, ladder=ladder, range_irreps=range_irreps)


def reference(trial_slab, ladder, range_irreps):
    block = CD // N_NARROW
    ranges = ladder.reshape(N_PAIR, AB_DEV, N_NARROW, block)

    def one_range(inputs):
        weights, label = inputs
        slab = lax.dynamic_index_in_dim(trial_slab, label, 0, keepdims=False)
        slab = slab.reshape(ROWS, N_NARROW, block).astype(jnp.float32)
        partial_value = jnp.einsum("rnc,anc->nra", slab, weights.astype(jnp.float32))
        rounded = lax.optimization_barrier(partial_value.astype(jnp.bfloat16)).astype(jnp.float32)
        return jnp.sum(rounded, axis=0).astype(jnp.bfloat16)

    pieces = lax.map(one_range, (ranges, range_irreps))
    return jnp.transpose(pieces, (1, 0, 2)).reshape(ROWS, AB)
```

```python
import functools

import jax
import jax.numpy as jnp
from jax import lax
from jax.experimental import pallas as pl
from jax.experimental.pallas import tpu as pltpu
from jax.sharding import PartitionSpec as P

MESH = pl.DeviceIdType.MESH
NT = (((1,), (1,)), ((), ()))


def kernel(
    pairs, narrows, chunks, group,
    irrep_ref, trial_hbm, ladder_hbm, out_ref,
    trial, chosen, arrived, ladder, acc, partial, parts, total, summed, owned,
    trial_sem, ladder_sem, send1, recv1, send2, recv2, send3, recv3,
):
    p, n = lax.axis_index("pair"), lax.axis_index("narrow")
    rows, width, own_rows = trial.shape[1], ladder.shape[2], trial.shape[1] // narrows
    local, lanes = ladder.shape[1], ladder.shape[1] // 128

    trial_copy = pltpu.make_async_copy(trial_hbm, trial, trial_sem)
    trial_copy.start()
    barrier = pltpu.get_barrier_semaphore()
    for d in range(1, pairs):
        pl.semaphore_signal(barrier, inc=1, device_id=(lax.rem(p + d, pairs), n), device_id_type=MESH)
    for d in range(1, narrows):
        pl.semaphore_signal(barrier, inc=1, device_id=(p, lax.rem(n + d, narrows)), device_id_type=MESH)
    ladder_copies = [
        pltpu.make_async_copy(ladder_hbm.at[:, pl.ds(c * width, width)], ladder.at[c], ladder_sem.at[c])
        for c in range(chunks)
    ]
    for copy in ladder_copies:
        copy.start()

    trial_copy.wait()
    for c in range(chunks):
        for q in range(pairs):
            chosen[c, q] = trial[irrep_ref[q], :, pl.ds(c * width, width)]
        arrived[c, p] = trial[irrep_ref[p], :, pl.ds(c * width, width)]
    pl.semaphore_wait(barrier, pairs + narrows - 2)

    def exchange(c, d):
        q = lax.rem(p + d, pairs)
        return pltpu.make_async_remote_copy(
            src_ref=chosen.at[c, q], dst_ref=arrived.at[c, p],
            send_sem=send1.at[c, d], recv_sem=recv1.at[c, d],
            device_id=(q, n), device_id_type=MESH,
        )

    for c in range(chunks):
        for d in range(1, pairs):
            exchange(c, d).start()

    for c in range(chunks):
        ladder_copies[c].wait()
        for d in range(1, pairs):
            exchange(c, d).wait_recv()

        def multiply(g):
            taken = arrived[c, pl.ds(g * group, group)].astype(jnp.float32)
            taken = taken.reshape(group * rows, width).astype(jnp.bfloat16)
            product = lax.dot_general(taken, ladder[c], NT, preferred_element_type=jnp.float32)
            at = pl.ds(g * group * rows, group * rows)
            for j in range(lanes):
                tile = product[:, j * 128:(j + 1) * 128]
                acc[j, at, :] = tile if c == 0 else acc[j, at, :] + tile

        if pairs == group:
            multiply(0)
        else:
            pl.loop(0, pairs // group)(multiply)

    for m in range(narrows):
        for j in range(lanes):
            piece = [acc[j, pl.ds(m * own_rows + k, pairs, stride=rows), :] for k in range(own_rows)]
            partial[m, j] = jnp.concatenate(piece, axis=0).astype(jnp.bfloat16)

    def reduce(d):
        m = lax.rem(n + d, narrows)
        return pltpu.make_async_remote_copy(
            src_ref=partial.at[m], dst_ref=parts.at[d],
            send_sem=send2.at[d], recv_sem=recv2.at[d],
            device_id=(p, m), device_id_type=MESH,
        )

    for d in range(1, narrows):
        reduce(d).start()
    value = partial[n].astype(jnp.float32)
    for d in range(1, narrows):
        reduce(d).wait_recv()
        value += parts[d].astype(jnp.float32)
    total[...] = value

    for q in range(pairs):
        for j in range(lanes):
            rounded = total[j, pl.ds(q, own_rows, stride=pairs), :].astype(jnp.bfloat16)
            summed[q, :, pl.ds(j * 128, 128)] = rounded

    def deliver(d):
        q = lax.rem(p + d, pairs)
        return pltpu.make_async_remote_copy(
            src_ref=summed.at[q], dst_ref=owned.at[p],
            send_sem=send3.at[d], recv_sem=recv3.at[d],
            device_id=(q, n), device_id_type=MESH,
        )

    for d in range(1, pairs):
        deliver(d).start()
    owned[p] = summed[p]
    for d in range(1, pairs):
        deliver(d).wait_recv()
    for q in range(pairs):
        out_ref[:, pl.ds(q * local, local)] = owned[q]

    for d in range(1, pairs):
        for c in range(chunks):
            exchange(c, d).wait_send()
        deliver(d).wait_send()
    for d in range(1, narrows):
        reduce(d).wait_send()


def body(trial_slab, ladder, range_irreps):
    pairs, narrows = lax.axis_size("pair"), lax.axis_size("narrow")
    irreps, rows, contracted = trial_slab.shape
    local = ladder.shape[0]
    chunks = 5 if contracted % (5 * 256) == 0 else 1
    width = contracted // chunks
    own_rows = rows // narrows
    group = min(pairs, max(1, 64 // rows))
    bf16, f32 = jnp.bfloat16, jnp.float32
    return pl.pallas_call(
        functools.partial(kernel, pairs, narrows, chunks, group),
        out_shape=jax.ShapeDtypeStruct((own_rows, pairs * local), bf16),
        in_specs=[
            pl.BlockSpec(memory_space=pltpu.SMEM),
            pl.BlockSpec(memory_space=pl.ANY),
            pl.BlockSpec(memory_space=pl.ANY),
        ],
        out_specs=pl.BlockSpec(memory_space=pltpu.VMEM),
        scratch_shapes=[
            pltpu.VMEM((irreps, rows, contracted), bf16),
            pltpu.VMEM((chunks, pairs, rows, width), bf16),
            pltpu.VMEM((chunks, pairs, rows, width), bf16),
            pltpu.VMEM((chunks, local, width), bf16),
            pltpu.VMEM((local // 128, pairs * rows, 128), f32),
            pltpu.VMEM((narrows, local // 128, own_rows * pairs, 128), bf16),
            pltpu.VMEM((narrows, local // 128, own_rows * pairs, 128), bf16),
            pltpu.VMEM((local // 128, own_rows * pairs, 128), f32),
            pltpu.VMEM((pairs, own_rows, local), bf16),
            pltpu.VMEM((pairs, own_rows, local), bf16),
            pltpu.SemaphoreType.DMA,
            pltpu.SemaphoreType.DMA((chunks,)),
            pltpu.SemaphoreType.DMA((chunks, pairs)),
            pltpu.SemaphoreType.DMA((chunks, pairs)),
            pltpu.SemaphoreType.DMA((narrows,)),
            pltpu.SemaphoreType.DMA((narrows,)),
            pltpu.SemaphoreType.DMA((pairs,)),
            pltpu.SemaphoreType.DMA((pairs,)),
        ],
        compiler_params=pltpu.CompilerParams(
            collective_id=0, has_side_effects=True, vmem_limit_bytes=48 * 1024 * 1024
        ),
    )(range_irreps, trial_slab, ladder)


def solution(mesh):
    placed = (P(None, "pair", "narrow"), P("pair", "narrow"), P())
    return jax.shard_map(
        body, mesh=mesh, in_specs=placed, out_specs=P(("pair", "narrow"), None), check_vma=False
    )
```

```python
import functools

import jax
import jax.numpy as jnp
from jax import lax
from jax.experimental import pallas as pl
from jax.experimental.pallas import tpu as pltpu
from jax.sharding import PartitionSpec as P

MESH = pl.DeviceIdType.MESH
NT = (((1,), (1,)), ((), ()))


def every(count, step):
    if count <= 8:
        for i in range(count):
            step(i)
    else:
        pl.loop(0, count)(step)


def kernel(
    pairs, narrows, chunks, group,
    irrep_hbm, trial_hbm, ladder_hbm, out_ref,
    irrep_ref, trial, chosen, arrived, ladder, acc, partial, parts, total,
    irrep_sem, trial_sem, ladder_sem, send1, recv1, send2, recv2,
):
    p, n = lax.axis_index("pair"), lax.axis_index("narrow")
    rows, width, own_rows = trial.shape[1], ladder.shape[2], trial.shape[1] // narrows
    local, lanes = ladder.shape[1], ladder.shape[1] // 128

    def each(step):
        every(narrows - 1, lambda e: step(0, e + 1))
        every(pairs - 1, lambda d: every(narrows, lambda e: step(d + 1, e)))

    def greet(d, e):
        peer = (lax.rem(p + d, pairs), lax.rem(n + e, narrows))
        pl.semaphore_signal(barrier, inc=1, device_id=peer, device_id_type=MESH)

    irrep_copy = pltpu.make_async_copy(irrep_hbm, irrep_ref, irrep_sem)
    irrep_copy.start()
    trial_copy = pltpu.make_async_copy(trial_hbm, trial, trial_sem)
    trial_copy.start()
    barrier = pltpu.get_barrier_semaphore()
    each(greet)
    ladder_copies = [
        pltpu.make_async_copy(ladder_hbm.at[:, pl.ds(c * width, width)], ladder.at[c], ladder_sem.at[c])
        for c in range(chunks)
    ]
    for copy in ladder_copies:
        copy.start()

    irrep_copy.wait()
    trial_copy.wait()
    for c in range(chunks):
        for q in range(pairs):
            chosen[c, q] = trial[irrep_ref[q], :, pl.ds(c * width, width)]
        arrived[c, p] = trial[irrep_ref[p], :, pl.ds(c * width, width)]
    pl.semaphore_wait(barrier, pairs * narrows - 1)

    def exchange(c, d):
        q = lax.rem(p + d, pairs)
        return pltpu.make_async_remote_copy(
            src_ref=chosen.at[c, q], dst_ref=arrived.at[c, p],
            send_sem=send1.at[c, d], recv_sem=recv1.at[c, d],
            device_id=(q, n), device_id_type=MESH,
        )

    for c in range(chunks):
        every(pairs - 1, lambda d: exchange(c, d + 1).start())

    for c in range(chunks):
        ladder_copies[c].wait()
        every(pairs - 1, lambda d: exchange(c, d + 1).wait_recv())

        def multiply(g):
            taken = arrived[c, pl.ds(g * group, group)].astype(jnp.float32)
            taken = taken.reshape(group * rows, width).astype(jnp.bfloat16)
            product = lax.dot_general(taken, ladder[c], NT, preferred_element_type=jnp.float32)
            for j in range(lanes):
                at = pl.ds(j * pairs * rows + g * group * rows, group * rows)
                tile = product[:, j * 128:(j + 1) * 128]
                acc[at, :] = tile if c == 0 else acc[at, :] + tile

        if pairs == group:
            multiply(0)
        else:
            pl.loop(0, pairs // group)(multiply)

    def pieces(q, m):
        first = q * rows + m * own_rows
        piece = [acc[pl.ds(first + k, lanes, stride=pairs * rows), :] for k in range(own_rows)]
        partial[q, m] = jnp.concatenate(piece, axis=0).astype(jnp.bfloat16)

    def deliver(d, e):
        q, m = lax.rem(p + d, pairs), lax.rem(n + e, narrows)
        return pltpu.make_async_remote_copy(
            src_ref=partial.at[q, m], dst_ref=parts.at[p, n],
            send_sem=send2.at[d, e], recv_sem=recv2.at[d, e],
            device_id=(q, m), device_id_type=MESH,
        )

    every(pairs, lambda q: every(narrows, lambda m: pieces(q, m)))
    each(lambda d, e: deliver(d, e).start())
    parts[p, n] = partial[p, n]
    each(lambda d, e: deliver(d, e).wait_recv())

    def add(q):
        value = parts[q, 0].astype(jnp.float32)
        for m in range(1, narrows):
            value += parts[q, m].astype(jnp.float32)
        total[q] = value
        for j in range(lanes):
            at = pl.ds(pl.multiple_of(q * local + j * 128, 128), 128)
            out_ref[:, at] = total[q, pl.ds(j, own_rows, stride=lanes), :].astype(jnp.bfloat16)

    every(pairs, add)

    for c in range(chunks):
        every(pairs - 1, lambda d: exchange(c, d + 1).wait_send())
    each(lambda d, e: deliver(d, e).wait_send())


def body(trial_slab, ladder, range_irreps):
    pairs, narrows = lax.axis_size("pair"), lax.axis_size("narrow")
    irreps, rows, contracted = trial_slab.shape
    local = ladder.shape[0]
    chunks = 5 if contracted % (5 * 256) == 0 else 1
    width = contracted // chunks
    own_rows = rows // narrows
    group = min(pairs, max(1, 64 // rows))
    bf16, f32 = jnp.bfloat16, jnp.float32
    return pl.pallas_call(
        functools.partial(kernel, pairs, narrows, chunks, group),
        out_shape=jax.ShapeDtypeStruct((own_rows, pairs * local), bf16),
        in_specs=[pl.BlockSpec(memory_space=pltpu.HBM)] * 3,
        out_specs=pl.BlockSpec(memory_space=pltpu.VMEM),
        scratch_shapes=[
            pltpu.SMEM(range_irreps.shape, jnp.int32),
            pltpu.VMEM((irreps, rows, contracted), bf16),
            pltpu.VMEM((chunks, pairs, rows, width), bf16),
            pltpu.VMEM((chunks, pairs, rows, width), bf16),
            pltpu.VMEM((chunks, local, width), bf16),
            pltpu.VMEM((local // 128 * pairs * rows, 128), f32),
            pltpu.VMEM((pairs, narrows, own_rows * local // 128, 128), bf16),
            pltpu.VMEM((pairs, narrows, own_rows * local // 128, 128), bf16),
            pltpu.VMEM((pairs, own_rows * local // 128, 128), f32),
            pltpu.SemaphoreType.DMA,
            pltpu.SemaphoreType.DMA,
            pltpu.SemaphoreType.DMA((chunks,)),
            pltpu.SemaphoreType.DMA((chunks, pairs)),
            pltpu.SemaphoreType.DMA((chunks, pairs)),
            pltpu.SemaphoreType.DMA((pairs, narrows)),
            pltpu.SemaphoreType.DMA((pairs, narrows)),
        ],
        compiler_params=pltpu.CompilerParams(
            collective_id=0, has_side_effects=True, vmem_limit_bytes=60 * 1024 * 1024
        ),
    )(range_irreps, trial_slab, ladder)


def solution(mesh):
    placed = (P(None, "pair", "narrow"), P("pair", "narrow"), P())
    return jax.shard_map(
        body, mesh=mesh, in_specs=placed, out_specs=P(("pair", "narrow"), None), check_vma=False
    )
```
